32 devices in a mesh: dom: 16 (over z, y, core), sub: 2 (over x).
Axes of the slice: x: 2, y: 2, z: 4, core: 2. Of those that a mesh axis runs over, the one named last changes fastest.
Arguments:
- fields: float32 [6, 56, 8192], P(None, None, ('dom', 'sub')), may hold values from -6 to 6
- metric: float32 [9, 8192], P(None, ('dom', 'sub')), may hold values from -4 to 4
- face_geom: float32 [4, 4, 8192], P(None, None, ('dom', 'sub')), as said below
- jacobian_ratio: float32 [56, 8192], P(None, ('dom', 'sub')), may hold values from 0.5 to 2
- curved: int32 [8192], P(('dom', 'sub')), may hold values 0 or 1
- derivatives: float32 [3, 56, 56], replicated, may hold values from -0.75 to 0.75
- lift_matrix: float32 [56, 84], replicated, may hold values from -0.625 to 0.625
- live_count: int32 [32], P(('dom', 'sub')), may hold values from 128 to 256, as said below
- send_list: int32 [32, 3, 2, 32], P(('dom', 'sub')), may hold values from 0 to 1023, as said below
- face_source: int32 [4, 8192], P(None, ('dom', 'sub')), may hold values from 0 to 1215, as said below
- face_permutation: int32 [4, 8192], P(None, ('dom', 'sub')), may hold values from 0 to 5
Outputs:
- advanced: float32 [6, 56, 8192], P(None, None, ('dom', 'sub'))
- section_register: float32 [6, 56, 8192], P(None, None, ('dom', 'sub'))
The draws below stay inside these ranges and needn't reach their ends.
Inputs may be any that keep to these rules, and one draw needn't show every extreme that they name: `live_count`: some device owns exactly 256 elements. `send_list`: each entry names a face f * 256 + e of an element that its device owns. `face_source`: an entry below 1024 names a face of an owned element of the same device; a larger entry names a ghost slot, never one whose source group lies outside the mesh. `face_geom`: unit normals and a positive surface scale.
All inputs are finite; a program needn't handle non-finite values. No bound on the sum of `curved` on one device may be relied on, other than what follows from the above.
Results may differ from the reference program's by a relative error of at most 0.0003.
Values sent between devices are 32-bit elements; how exact they have to be, the bound alone decides.
A program may use at most 128 MiB of HBM per device.

```python
import math
import jax
import jax.numpy as jnp
import numpy as np
from jax import lax

NP = 56
NFP = 21
E_DEV = 256
CAP = 32
ELEMS = 8192
N_DOM = 16
N_SUB = 2


def live_counts(key):
    device_total = N_DOM * N_SUB
    count_key, full_key = jax.random.split(jax.random.fold_in(key, 11))
    counts = jax.random.randint(count_key, (device_total,), E_DEV // 2, E_DEV + 1)
    fullest = jax.random.randint(full_key, (), 0, device_total)
    return jnp.where(jnp.arange(device_total) == fullest, E_DEV, counts).astype(jnp.int32)


def peer_counts(key):
    device_total = N_DOM * N_SUB
    count_key, full_key = jax.random.split(jax.random.fold_in(key, 23))
    counts = jax.random.randint(count_key, (device_total, 3, N_SUB), CAP // 4, 3 * CAP // 4 + 1)
    target = jax.random.randint(full_key, (device_total,), 0, N_SUB)
    group_ids = jnp.arange(device_total, dtype=jnp.int32) // N_SUB
    chosen_offset = jnp.where(group_ids < N_DOM - 1, 2, 1)
    offsets = jnp.arange(3, dtype=jnp.int32)[None, :, None]
    sub_ids = jnp.arange(N_SUB, dtype=jnp.int32)[None, None, :]
    full_mask = (offsets == chosen_offset[:, None, None]) & (sub_ids == target[:, None, None])
    counts = jnp.where(full_mask, CAP, counts)
    edge_mask = (offsets == 0) & (group_ids[:, None, None] == 0) | (offsets == 2) & (group_ids[:, None, None] == N_DOM - 1)
    return jnp.where(edge_mask, 0, counts).astype(jnp.int32)


def draw_live_count(key, part):
    return live_counts(key)


def draw_send_list(key, part):
    device_total = N_DOM * N_SUB
    live_sizes = live_counts(key)
    face_key, elem_key = jax.random.split(jax.random.fold_in(key, 31))
    grid_shape = (device_total, 3, N_SUB, CAP)
    face_ids = jax.random.randint(face_key, grid_shape, 0, 4)
    elem_ids = jax.random.randint(elem_key, grid_shape, 0, live_sizes[:, None, None, None])
    return (face_ids * E_DEV + elem_ids).astype(jnp.int32)


def draw_face_source(key, part):
    device_total = N_DOM * N_SUB
    slot_total = 3 * N_SUB * CAP
    face_total = 4 * E_DEV
    live_sizes = live_counts(key)
    counts = peer_counts(key)
    device_ids = jnp.arange(device_total, dtype=jnp.int32)
    group_ids = device_ids // N_SUB
    own_sub = device_ids % N_SUB
    offsets = jnp.arange(3, dtype=jnp.int32)[None, :, None]
    sub_ids = jnp.arange(N_SUB, dtype=jnp.int32)[None, None, :]
    source_group = group_ids[:, None, None] - offsets + 1
    valid_mask = (source_group >= 0) & (source_group < N_DOM)
    sender = jnp.clip(source_group, 0, N_DOM - 1) * N_SUB + sub_ids
    incoming = counts[sender, offsets + 0 * sub_ids, own_sub[:, None, None] + 0 * sub_ids] * valid_mask
    slot_live = (jnp.arange(CAP, dtype=jnp.int32)[None, None, None, :] < incoming[..., None]).reshape(device_total, slot_total).astype(jnp.int32)
    slot_key, face_key, pick_face, pick_elem = jax.random.split(jax.random.fold_in(key, 47), 4)
    slot_perm = jax.vmap(lambda k: jax.random.permutation(k, slot_total))(jax.random.split(slot_key, device_total))
    slot_order = jnp.argsort((1 - slot_live) * slot_total + slot_perm, axis=1)
    live_slots = jnp.sum(slot_live, axis=1)
    face_elem = jnp.arange(face_total, dtype=jnp.int32) % E_DEV
    dead_face = (face_elem[None, :] >= live_sizes[:, None]).astype(jnp.int32)
    face_perm = jax.vmap(lambda k: jax.random.permutation(k, face_total))(jax.random.split(face_key, device_total))
    face_rank = jnp.argsort(jnp.argsort(dead_face * face_total + face_perm, axis=1), axis=1)
    remote = face_rank < live_slots[:, None]
    chosen = jnp.take_along_axis(slot_order, jnp.clip(face_rank, 0, slot_total - 1), axis=1)
    local_face = jax.random.randint(pick_face, (device_total, face_total), 0, 4) * E_DEV + jax.random.randint(pick_elem, (device_total, face_total), 0, live_sizes[:, None])
    source = jnp.where(remote, face_total + chosen, local_face)
    return jnp.transpose(source.reshape(device_total, 4, E_DEV), (1, 0, 2)).reshape(4, device_total * E_DEV).astype(jnp.int32)


def draw_face_geom(key, part):
    subkeys = jax.random.split(key, 3)
    grid_shape = (4, ELEMS)
    polar_angle = jnp.arccos(jax.random.uniform(subkeys[0], grid_shape, jnp.float32, -1.0, 1.0))
    azimuth = jax.random.uniform(subkeys[1], grid_shape, jnp.float32, -math.pi, math.pi)
    face_scale = jnp.exp(jax.random.uniform(subkeys[2], grid_shape, jnp.float32, 0.0, math.log(4.0)))
    return jnp.stack([jnp.sin(polar_angle) * jnp.cos(azimuth), jnp.sin(polar_angle) * jnp.sin(azimuth), jnp.cos(polar_angle), face_scale], axis=0).astype(jnp.float32)


def with_ends(values, stream_key, smallest, high):
    longest = values.shape.index(max(values.shape))
    spots = []
    for shift in (0, 1):
        where = [jax.random.randint(jax.random.fold_in(stream_key, axis), (), 0, length) for axis, length in enumerate(values.shape)]
        where[longest] = (where[longest] + shift) % values.shape[longest]
        spots.append(tuple(where))
    return values.at[spots[0]].set(smallest).at[spots[1]].set(high)


def shard_levels(own_key, shape, cuts, low, high):
    def one(axis_at, parts):
        draws = jax.random.uniform(jax.random.fold_in(jax.random.fold_in(own_key, 6), axis_at), (parts,), jnp.float32, low / len(cuts), high / len(cuts))
        return jnp.repeat(jnp.exp(draws), shape[axis_at] // parts).reshape((-1,) + (1,) * (len(shape) - axis_at - 1))

    loudness = one(*cuts[0])
    for cut in cuts[1:]:
        loudness = loudness * one(*cut)
    return loudness


def gaussian(rng, extent, deviation, most, cuts=(), held_as=jnp.bfloat16):
    gain = shard_levels(rng, extent, cuts, -0.22, 0.18) if cuts else 1.0
    entries = jax.random.normal(rng, extent, jnp.float32) * deviation * gain
    return jnp.minimum(jnp.maximum(entries, -most), most).astype(held_as)


def setup_inputs(seed: int = 0) -> dict:
    streams_of = jax.random.split(jax.random.key(seed), 12)
    return {
        "fields": gaussian(streams_of[0], (6, NP, ELEMS), 1.0, 6.0, ((2, 32),), jnp.float32),
        "metric": gaussian(streams_of[1], (9, ELEMS), 1.0, 4.0, ((1, 32),), jnp.float32),
        "face_geom": draw_face_geom(jax.random.fold_in(streams_of[11], 71), 0),
        "jacobian_ratio": jnp.clip(0.5 + 1.5 * jax.random.uniform(streams_of[3], (NP, ELEMS), jnp.float32) ** shard_levels(streams_of[3], (NP, ELEMS), ((1, 32),), -0.2, 0.2), 0.5, 2.0),
        "curved": with_ends((jax.random.randint(streams_of[4], (ELEMS,), 0, 4) < 1).astype(jnp.int32), jax.random.fold_in(streams_of[4], 1), 0, 1),
        "derivatives": gaussian(streams_of[5], (3, NP, NP), NP ** -0.5, 0.75, (), jnp.float32),
        "lift_matrix": gaussian(streams_of[6], (NP, 4 * NFP), (4 * NFP) ** -0.5, 0.625, (), jnp.float32),
        "live_count": draw_live_count(jax.random.fold_in(streams_of[11], 71), 0),
        "send_list": draw_send_list(jax.random.fold_in(streams_of[11], 71), 0),
        "face_source": draw_face_source(jax.random.fold_in(streams_of[11], 71), 0),
        "face_permutation": with_ends(jax.random.randint(streams_of[10], (4, ELEMS), 0, 6), jax.random.fold_in(streams_of[10], 1), 0, 5).astype(jnp.int32),
    }


RK_A = (0.0, -567301805773.0 / 1357537059087.0)
RK_B = (1432997174477.0 / 9575080441755.0, 5161836677717.0 / 13612068292357.0)
TIME_STEP = 0.5
SYMMETRIES = ((0, 1, 2), (1, 2, 0), (2, 0, 1), (0, 2, 1), (2, 1, 0), (1, 0, 2))


def node_tables():
    volume_nodes = [(i, j, k) for i in range(6) for j in range(6 - i) for k in range(6 - i - j)]
    volume_index = {v: n for n, v in enumerate(volume_nodes)}
    triangle = [(a, b) for a in range(6) for b in range(6 - a)]
    triangle_index = {t: n for n, t in enumerate(triangle)}
    face_nodes = np.array([[volume_index[(a, b, 0)] for a, b in triangle],
                           [volume_index[(a, 0, b)] for a, b in triangle],
                           [volume_index[(a, b, 5 - a - b)] for a, b in triangle],
                           [volume_index[(0, a, b)] for a, b in triangle]], np.int32)
    permuted = np.array([[triangle_index[((a, b, 5 - a - b)[q[0]], (a, b, 5 - a - b)[q[1]])] for a, b in triangle]
                         for q in SYMMETRIES], np.int32)
    return face_nodes, permuted


def volume_and_flux(current, exterior, interior, metric, face_geom, derivatives):
    slopes = jnp.einsum("mpq,cqe->mcpe", derivatives, current, precision=lax.Precision.HIGHEST)
    gradients = [metric[x] * slopes[0] + metric[3 + x] * slopes[1] + metric[6 + x] * slopes[2] for x in range(3)]
    diff_x, diff_y, diff_z = gradients
    volume = jnp.stack([
        -(diff_y[5] - diff_z[4]), -(diff_z[3] - diff_x[5]), -(diff_x[4] - diff_y[3]),
        diff_y[2] - diff_z[1], diff_z[0] - diff_x[2], diff_x[1] - diff_y[0]])
    jump = exterior - interior
    normal_x, normal_y, normal_z, face_scale = face_geom[0], face_geom[1], face_geom[2], face_geom[3]
    along_h = normal_x * jump[0] + normal_y * jump[1] + normal_z * jump[2]
    along_e = normal_x * jump[3] + normal_y * jump[4] + normal_z * jump[5]
    flux_all = jnp.stack([
        -(normal_y * jump[5] - normal_z * jump[4]) + jump[0] - along_h * normal_x,
        -(normal_z * jump[3] - normal_x * jump[5]) + jump[1] - along_h * normal_y,
        -(normal_x * jump[4] - normal_y * jump[3]) + jump[2] - along_h * normal_z,
        (normal_y * jump[2] - normal_z * jump[1]) + jump[3] - along_e * normal_x,
        (normal_z * jump[0] - normal_x * jump[2]) + jump[4] - along_e * normal_y,
        (normal_x * jump[1] - normal_y * jump[0]) + jump[5] - along_e * normal_z]) * (0.5 * face_scale)
    return volume, flux_all


def reference(fields, metric, face_geom, jacobian_ratio, curved, derivatives, lift_matrix, live_count, send_list, face_source, face_permutation):
    face_nodes, permuted = node_tables()
    node_table = jnp.asarray(face_nodes)
    turn_table = jnp.asarray(permuted)
    device_total = N_DOM * N_SUB
    local_ids = jnp.arange(E_DEV, dtype=jnp.int32)
    alive_all = (local_ids[None, :] < live_count[:, None]).astype(fields.dtype).reshape(-1)
    current = fields * alive_all
    residual = jnp.zeros_like(fields)
    offsets = jnp.arange(3, dtype=jnp.int32)[:, None, None]
    sub_ids = jnp.arange(N_SUB, dtype=jnp.int32)[None, :, None]
    lanes = jnp.arange(CAP, dtype=jnp.int32)[None, None, :]
    lift_three = lift_matrix.reshape(NP, 4, NFP)
    for step_index in range(2):
        def receive(device):
            group_id = device // N_SUB
            sub_id = device % N_SUB
            source_group = group_id - offsets + 1
            valid_mask = ((source_group >= 0) & (source_group < N_DOM)).astype(fields.dtype)
            sender = jnp.broadcast_to(jnp.clip(source_group, 0, N_DOM - 1) * N_SUB + sub_ids, (3, N_SUB, CAP))
            picked = send_list[sender, offsets + 0 * lanes, sub_id, lanes + 0 * sub_ids]
            face_id = picked // E_DEV
            elem_id = picked % E_DEV + sender * E_DEV
            node_index = node_table[face_id]
            values = current[:, node_index, elem_id[..., None]]
            values = values * valid_mask[None, :, :, :, None]
            return jnp.moveaxis(values, 4, 1).reshape(6, NFP, 3 * N_SUB * CAP)

        def evaluate(device):
            start = device * E_DEV
            block = lax.dynamic_slice_in_dim(current, start, E_DEV, 2)
            metric_block = lax.dynamic_slice_in_dim(metric, start, E_DEV, 1)
            geom_block = lax.dynamic_slice_in_dim(face_geom, start, E_DEV, 2)
            ratio_block = lax.dynamic_slice_in_dim(jacobian_ratio, start, E_DEV, 1)
            curved_block = lax.dynamic_slice_in_dim(curved, start, E_DEV, 0)
            source_block = lax.dynamic_slice_in_dim(face_source, start, E_DEV, 1)
            turn_block = lax.dynamic_slice_in_dim(face_permutation, start, E_DEV, 1)
            alive_block = lax.dynamic_slice_in_dim(alive_all, start, E_DEV, 0)
            interior = block[:, node_table.T, :]
            table = jnp.concatenate([interior.reshape(6, NFP, 4 * E_DEV), receive(device)], axis=2)
            gathered = jnp.take(table, source_block.reshape(-1), axis=2).reshape(6, NFP, 4, E_DEV)
            turn_index = jnp.transpose(turn_table[turn_block], (2, 0, 1))
            exterior = jnp.take_along_axis(gathered, turn_index[None], axis=1)
            volume, flux_all = volume_and_flux(block, exterior, interior, metric_block, geom_block, derivatives)
            lifted = jnp.einsum("nfi,cife->cne", lift_three, flux_all, precision=lax.Precision.HIGHEST)
            scaling = jnp.where(curved_block == 1, ratio_block, 1.0) * alive_block
            return (volume + lifted) * scaling

        rate = lax.map(evaluate, jnp.arange(device_total, dtype=jnp.int32))
        rate = jnp.transpose(rate, (1, 2, 0, 3)).reshape(6, NP, device_total * E_DEV)
        residual = RK_A[step_index] * residual + TIME_STEP * rate
        current = current + RK_B[step_index] * residual
    return current, residual
```

```python
import functools

import jax
import jax.numpy as jnp
import numpy as np
from jax import lax
from jax.experimental import pallas as pl
from jax.experimental.pallas import tpu as pltpu
from jax.sharding import PartitionSpec as P

RK_A = (0.0, -567301805773.0 / 1357537059087.0)
RK_B = (1432997174477.0 / 9575080441755.0, 5161836677717.0 / 13612068292357.0)
TIME_STEP = 0.5
SYMMETRIES = ((0, 1, 2), (1, 2, 0), (2, 0, 1), (0, 2, 1), (2, 1, 0), (1, 0, 2))
F32 = jnp.float32
BF16 = jnp.bfloat16
NODES = 56
TRACE = 21
ROWS = 24
GROUP = 3 * ROWS
PAIR = 2 * GROUP
LANES = 128
MESH = pl.DeviceIdType.MESH


def node_tables():
    volume_nodes = [(i, j, k) for i in range(6) for j in range(6 - i) for k in range(6 - i - j)]
    volume_index = {v: n for n, v in enumerate(volume_nodes)}
    triangle = [(a, b) for a in range(6) for b in range(6 - a)]
    triangle_index = {t: n for n, t in enumerate(triangle)}
    face_nodes = np.array(
        [
            [volume_index[a, b, 0] for a, b in triangle],
            [volume_index[a, 0, b] for a, b in triangle],
            [volume_index[a, b, 5 - a - b] for a, b in triangle],
            [volume_index[0, a, b] for a, b in triangle],
        ],
        np.int32,
    )
    permuted = np.array(
        [
            [triangle_index[(a, b, 5 - a - b)[q[0]], (a, b, 5 - a - b)[q[1]]] for a, b in triangle]
            for q in SYMMETRIES
        ],
        np.int32,
    )
    return (face_nodes, permuted)


def zero_one_matrices():
    face_nodes, permuted = node_tables()
    pick = np.zeros((4 * ROWS, NODES), np.float32)
    spread = np.zeros((4 * TRACE, 4 * ROWS), np.float32)
    for f in range(4):
        for m in range(TRACE):
            pick[f * ROWS + m, face_nodes[f, m]] = 1
            spread[f * TRACE + m, f * ROWS + m] = 1
    turn = np.zeros((5 * GROUP, PAIR), np.float32)
    for p in range(1, 6):
        for c in range(3):
            for m in range(TRACE):
                for part in range(2):
                    turn[(p - 1) * GROUP + c * ROWS + m, part * GROUP + c * ROWS + permuted[p, m]] = 1
    pack = np.zeros((2 * PAIR, LANES), np.float32)
    unpack = np.zeros((2 * GROUP, LANES), np.float32)
    for q in range(2):
        for c in range(3):
            for m in range(TRACE):
                lane = (3 * q + c) * TRACE + m
                unpack[q * GROUP + c * ROWS + m, lane] = 1
                for part in range(2):
                    pack[q * PAIR + part * GROUP + c * ROWS + m, lane] = 1
    return tuple(jnp.asarray(a, BF16) for a in (pick, spread, turn, pack, unpack))


def halves(x):
    high = x.astype(BF16)
    low = (x - high.astype(F32)).astype(BF16)
    return high, low


def dot(a, b):
    return jnp.dot(a, b, preferred_element_type=F32)


def dot_nt(a, b):
    return lax.dot_general(a, b, (((1,), (1,)), ((), ())), preferred_element_type=F32)


def kernel(
    n_dom,
    n_sub,
    live_ref,
    fields_ref,
    metric_ref,
    geom_ref,
    ratio_ref,
    curved_ref,
    deriv_ref,
    lift_ref,
    send_ref,
    source_ref,
    perm_ref,
    pick_ref,
    spread_ref,
    turn_ref,
    pack_ref,
    unpack_ref,
    adv_ref,
    reg_ref,
    table,
    inner,
    gathered,
    hot_local,
    hot_ghost,
    hot_send,
    out_buf,
    ghost,
    volume,
    scale,
    send_sem,
    recv_sem,
):
    elements = fields_ref.shape[2]
    faces = 4 * elements
    cap = send_ref.shape[2]
    slots = 3 * n_sub * cap
    g = lax.axis_index("dom")
    me = lax.axis_index("sub")
    below = g > 0
    above = g < n_dom - 1
    send_ok = (below, None, above)
    recv_ok = (above, None, below)

    def guarded(ok, act):
        if ok is None:
            act()
        else:
            pl.when(ok)(act)

    def peers(o):
        return [lax.rem(me + d, n_sub) for d in range(1 if o == 1 else 0, n_sub)]

    def rows(o, j):
        return pl.ds(pl.multiple_of((o * n_sub + j) * cap, cap), cap)

    barrier = pltpu.get_barrier_semaphore()
    for o in range(3):

        def greet(o=o):
            for j in peers(o):
                pl.semaphore_signal(barrier, inc=1, device_id=(g + o - 1, j), device_id_type=MESH)

        guarded(send_ok[o], greet)

    def copy(step, o, j):
        return pltpu.make_async_remote_copy(
            src_ref=out_buf.at[step, rows(o, j)],
            dst_ref=ghost.at[step, rows(o, me)],
            send_sem=send_sem.at[step, o, j],
            recv_sem=recv_sem.at[step, o, me],
            device_id=(g + o - 1, j),
            device_id_type=MESH,
        )

    def arrival(step, o, j):
        return pltpu.make_async_remote_copy(
            src_ref=out_buf.at[step, rows(o, j)],
            dst_ref=ghost.at[step, rows(o, j)],
            send_sem=send_sem.at[step, o, j],
            recv_sem=recv_sem.at[step, o, j],
            device_id=(g - o + 1, j),
            device_id_type=MESH,
        )

    square_r = lax.broadcasted_iota(jnp.int32, (cap, cap), 0)
    square_c = lax.broadcasted_iota(jnp.int32, (cap, cap), 1)
    face_lane = lax.broadcasted_iota(jnp.int32, (cap, faces), 1)
    for o in range(3):
        for j in range(n_sub):
            row = send_ref[o, j : j + 1, :]
            column = jnp.sum(jnp.where(square_r == square_c, row, 0), axis=1, keepdims=True)
            at = (o * n_sub + j) * cap
            hot_send[at : at + cap, :] = jnp.where(face_lane == column, 1.0, 0.0).astype(BF16)

    alive = lax.broadcasted_iota(jnp.int32, (1, elements), 1) < live_ref[0]

    for step in range(2):
        parts = []
        for c in range(6):
            if step == 0:
                u = jnp.where(alive, fields_ref[c], 0.0)
                adv_ref[c] = u
            else:
                u = adv_ref[c]
            parts.append(halves(u))
        pick = pick_ref[...]
        for q in range(2):
            high = [dot(pick, parts[3 * q + c][0]) for c in range(3)]
            low = [dot(pick, parts[3 * q + c][1]) for c in range(3)]
            for f in range(4):
                at = f * ROWS
                h = jnp.concatenate([x[at : at + ROWS] for x in high], axis=0)
                l = jnp.concatenate([x[at : at + ROWS] for x in low], axis=0)
                inner[q, f] = h + l
                table[q * PAIR : (q + 1) * PAIR, f * elements : (f + 1) * elements] = jnp.concatenate(
                    [h, l], axis=0
                ).astype(BF16)
        outgoing = dot_nt(hot_send[...], table[...])
        out_buf[step] = dot(outgoing.astype(BF16), pack_ref[...])

        if step == 0:
            for k in range(2):

                def blank_above(k=k):
                    ghost[k, 0 : n_sub * cap, :] = jnp.zeros((n_sub * cap, LANES), F32)

                def blank_below(k=k):
                    ghost[k, 2 * n_sub * cap :, :] = jnp.zeros((n_sub * cap, LANES), F32)

                pl.when(jnp.logical_not(above))(blank_above)
                pl.when(jnp.logical_not(below))(blank_below)
            sides = jnp.minimum(g, 1) + jnp.minimum(n_dom - 1 - g, 1)
            pl.semaphore_wait(barrier, n_sub * (sides + 1) - 1)
        for o in (2, 0, 1):

            def start(o=o):
                for j in peers(o):
                    copy(step, o, j).start()

            guarded(send_ok[o], start)
        ghost[step, rows(1, me), :] = out_buf[step, rows(1, me), :]

        if step == 0:
            local_row = lax.broadcasted_iota(jnp.int32, (faces, elements), 0)
            ghost_row = lax.broadcasted_iota(jnp.int32, (slots, elements), 0) + faces
            for f in range(4):
                source = source_ref[f : f + 1, :]
                lanes = slice(f * elements, (f + 1) * elements)
                hot_local[:, lanes] = jnp.where(local_row == source, 1.0, 0.0).astype(BF16)
                hot_ghost[:, lanes] = jnp.where(ghost_row == source, 1.0, 0.0).astype(BF16)
            ratio = jnp.where(curved_ref[...] == 1, ratio_ref[...], 1.0)
            scale[...] = jnp.where(alive, ratio, 0.0)
            deriv = deriv_ref[...].reshape(3 * NODES, NODES)
            deriv_high, deriv_low = halves(deriv)
            lift_high, lift_low = halves(lift_ref[...])
            lift_high = dot(lift_high, spread_ref[...]).astype(BF16)
            lift_low = dot(lift_low, spread_ref[...]).astype(BF16)

        def slope(c):
            high, low = parts[c]
            s = dot(deriv_high, high) + (dot(deriv_low, high) + dot(deriv_high, low))
            return s[0:NODES], s[NODES : 2 * NODES], s[2 * NODES :]

        def along(s, x):
            return (
                metric_ref[x : x + 1, :] * s[0]
                + metric_ref[3 + x : 4 + x, :] * s[1]
                + metric_ref[6 + x : 7 + x, :] * s[2]
            )

        for q in range(2):
            sx, sy, sz = slope(3 * q), slope(3 * q + 1), slope(3 * q + 2)
            curl = (
                along(sz, 1) - along(sy, 2),
                along(sx, 2) - along(sz, 0),
                along(sy, 0) - along(sx, 1),
            )
            for c in range(3):
                if q == 0:
                    volume[3 + c] = curl[c]
                else:
                    volume[c] = -curl[c]
        for f in range(4):
            lanes = slice(f * elements, (f + 1) * elements)
            gathered[:, lanes] = dot(table[...], hot_local[:, lanes])

        for o in range(3):

            def land(o=o):
                for j in peers(o):
                    arrival(step, o, j).wait_recv()

            guarded(recv_ok[o], land)

        ghost_high, ghost_low = halves(ghost[step])
        far_high = dot_nt(unpack_ref[...], ghost_high)
        far_low = dot_nt(unpack_ref[...], ghost_low)
        far = jnp.concatenate(
            [far_high[:GROUP], far_low[:GROUP], far_high[GROUP:], far_low[GROUP:]], axis=0
        ).astype(BF16)

        turn = turn_ref[...]
        flux = [[] for _ in range(6)]
        for f in range(4):
            lanes = slice(f * elements, (f + 1) * elements)
            outer = gathered[:, lanes] + dot(far, hot_ghost[:, lanes])
            symmetry = perm_ref[f : f + 1, :]
            jump = []
            for q in range(2):
                pair = outer[q * PAIR : (q + 1) * PAIR]
                turned = dot(turn, pair.astype(BF16))
                exterior = pair[:GROUP] + pair[GROUP:]
                for p in range(1, 6):
                    exterior = jnp.where(symmetry == p, turned[(p - 1) * GROUP : p * GROUP], exterior)
                difference = exterior - inner[q, f]
                jump += [difference[c * ROWS : (c + 1) * ROWS] for c in range(3)]
            nx, ny, nz = (geom_ref[k, f : f + 1, :] for k in range(3))
            half = 0.5 * geom_ref[3, f : f + 1, :]
            along_h = nx * jump[0] + ny * jump[1] + nz * jump[2]
            along_e = nx * jump[3] + ny * jump[4] + nz * jump[5]
            flux[0].append(half * (nz * jump[4] - ny * jump[5] + jump[0] - along_h * nx))
            flux[1].append(half * (nx * jump[5] - nz * jump[3] + jump[1] - along_h * ny))
            flux[2].append(half * (ny * jump[3] - nx * jump[4] + jump[2] - along_h * nz))
            flux[3].append(half * (ny * jump[2] - nz * jump[1] + jump[3] - along_e * nx))
            flux[4].append(half * (nz * jump[0] - nx * jump[2] + jump[4] - along_e * ny))
            flux[5].append(half * (nx * jump[1] - ny * jump[0] + jump[5] - along_e * nz))
        for c in range(6):
            high, low = halves(jnp.concatenate(flux[c], axis=0))
            lifted = dot(lift_high, high) + (dot(lift_low, high) + dot(lift_high, low))
            register = TIME_STEP * ((volume[c] + lifted) * scale[...])
            if step == 1:
                register = RK_A[1] * reg_ref[c] + register
            reg_ref[c] = register
            adv_ref[c] = adv_ref[c] + RK_B[step] * register

    for step in range(2):
        for o in range(3):

            def sent(o=o, step=step):
                for j in peers(o):
                    copy(step, o, j).wait_send()

            guarded(send_ok[o], sent)


def on_device(
    n_dom,
    n_sub,
    fields,
    metric,
    face_geom,
    jacobian_ratio,
    curved,
    derivatives,
    lift_matrix,
    live_count,
    send_list,
    face_source,
    face_permutation,
):
    elements = fields.shape[2]
    faces = 4 * elements
    slots = 3 * n_sub * send_list.shape[3]
    vmem = pl.BlockSpec(memory_space=pltpu.VMEM)
    smem = pl.BlockSpec(memory_space=pltpu.SMEM)
    shape = jax.ShapeDtypeStruct(fields.shape, F32)
    return pl.pallas_call(
        functools.partial(kernel, n_dom, n_sub),
        out_shape=(shape, shape),
        in_specs=[smem] + [vmem] * 15,
        out_specs=(vmem, vmem),
        scratch_shapes=[
            pltpu.VMEM((2 * PAIR, faces), BF16),
            pltpu.VMEM((2, 4, GROUP, elements), F32),
            pltpu.VMEM((2 * PAIR, faces), F32),
            pltpu.VMEM((faces, faces), BF16),
            pltpu.VMEM((slots, faces), BF16),
            pltpu.VMEM((slots, faces), BF16),
            pltpu.VMEM((2, slots, LANES), F32),
            pltpu.VMEM((2, slots, LANES), F32),
            pltpu.VMEM((6, NODES, elements), F32),
            pltpu.VMEM((NODES, elements), F32),
            pltpu.SemaphoreType.DMA((2, 3, n_sub)),
            pltpu.SemaphoreType.DMA((2, 3, n_sub)),
        ],
        compiler_params=pltpu.CompilerParams(
            collective_id=0, has_side_effects=True, vmem_limit_bytes=40 * 1024 * 1024
        ),
        cost_estimate=pl.CostEstimate(flops=4_000_000_000, bytes_accessed=2_000_000, transcendentals=0),
    )(
        live_count,
        fields,
        metric,
        face_geom,
        jacobian_ratio,
        curved.reshape(1, elements),
        derivatives,
        lift_matrix,
        send_list.reshape(send_list.shape[1:]),
        face_source,
        face_permutation,
        *zero_one_matrices(),
    )


def solution(mesh):
    return jax.shard_map(
        functools.partial(on_device, mesh.shape["dom"], mesh.shape["sub"]),
        mesh=mesh,
        in_specs=(
            P(None, None, ("dom", "sub")),
            P(None, ("dom", "sub")),
            P(None, None, ("dom", "sub")),
            P(None, ("dom", "sub")),
            P(("dom", "sub")),
            P(),
            P(),
            P(("dom", "sub")),
            P(("dom", "sub"), None, None, None),
            P(None, ("dom", "sub")),
            P(None, ("dom", "sub")),
        ),
        out_specs=(P(None, None, ("dom", "sub")), P(None, None, ("dom", "sub"))),
        check_vma=False,
    )
```

```python
import functools

import jax
import jax.numpy as jnp
import numpy as np
from jax import lax
from jax.experimental import pallas as pl
from jax.experimental.pallas import tpu as pltpu
from jax.sharding import PartitionSpec as P

RK_A = (0.0, -567301805773.0 / 1357537059087.0)
RK_B = (1432997174477.0 / 9575080441755.0, 5161836677717.0 / 13612068292357.0)
TIME_STEP = 0.5
SYMMETRIES = ((0, 1, 2), (1, 2, 0), (2, 0, 1), (0, 2, 1), (2, 1, 0), (1, 0, 2))
F32 = jnp.float32
BF16 = jnp.bfloat16
NODES = 56
TRACE = 21
ROWS = 24
GROUP = 3 * ROWS
PAIR = 2 * GROUP
LANES = 128
MESH = pl.DeviceIdType.MESH


def node_tables():
    volume_nodes = [(i, j, k) for i in range(6) for j in range(6 - i) for k in range(6 - i - j)]
    volume_index = {v: n for n, v in enumerate(volume_nodes)}
    triangle = [(a, b) for a in range(6) for b in range(6 - a)]
    triangle_index = {t: n for n, t in enumerate(triangle)}
    face_nodes = np.array(
        [
            [volume_index[a, b, 0] for a, b in triangle],
            [volume_index[a, 0, b] for a, b in triangle],
            [volume_index[a, b, 5 - a - b] for a, b in triangle],
            [volume_index[0, a, b] for a, b in triangle],
        ],
        np.int32,
    )
    permuted = np.array(
        [
            [triangle_index[(a, b, 5 - a - b)[q[0]], (a, b, 5 - a - b)[q[1]]] for a, b in triangle]
            for q in SYMMETRIES
        ],
        np.int32,
    )
    return (face_nodes, permuted)


def zero_one_matrices():
    face_nodes, permuted = node_tables()
    pick = np.zeros((4 * ROWS, NODES), np.float32)
    spread = np.zeros((4 * TRACE, 4 * ROWS), np.float32)
    for f in range(4):
        for m in range(TRACE):
            pick[f * ROWS + m, face_nodes[f, m]] = 1
            spread[f * TRACE + m, f * ROWS + m] = 1
    turn = np.zeros((5 * GROUP, PAIR), np.float32)
    for p in range(1, 6):
        for c in range(3):
            for m in range(TRACE):
                for part in range(2):
                    turn[(p - 1) * GROUP + c * ROWS + m, part * GROUP + c * ROWS + permuted[p, m]] = 1
    pack = np.zeros((2 * PAIR, LANES), np.float32)
    unpack = np.zeros((2 * GROUP, LANES), np.float32)
    for q in range(2):
        for c in range(3):
            for m in range(TRACE):
                lane = (3 * q + c) * TRACE + m
                unpack[q * GROUP + c * ROWS + m, lane] = 1
                for part in range(2):
                    pack[q * PAIR + part * GROUP + c * ROWS + m, lane] = 1
    return tuple(jnp.asarray(a, BF16) for a in (pick, spread, turn, pack, unpack))


def halves(x):
    high = x.astype(BF16)
    low = (x - high.astype(F32)).astype(BF16)
    return high, low


def dot(a, b):
    return jnp.dot(a, b, preferred_element_type=F32)


def dot_nt(a, b):
    return lax.dot_general(a, b, (((1,), (1,)), ((), ())), preferred_element_type=F32)


def lifted(lift, high, low):
    main = dot(lift, high)
    return main[:NODES] + (main[NODES:] + dot(lift, low)[:NODES])


def kernel(
    n_dom,
    n_sub,
    live_ref,
    fields_hbm,
    send_hbm,
    pick_hbm,
    pack_hbm,
    source_hbm,
    deriv_hbm,
    metric_hbm,
    curved_hbm,
    ratio_hbm,
    unpack_hbm,
    turn_hbm,
    perm_hbm,
    geom_hbm,
    lift_hbm,
    spread_hbm,
    adv_ref,
    reg_ref,
    volume,
    scale,
    flux_high,
    flux_low,
    lift_ref,
    send_ref,
    pick_ref,
    pack_ref,
    source_ref,
    deriv_ref,
    metric_ref,
    curved_ref,
    ratio_ref,
    unpack_ref,
    turn_ref,
    perm_ref,
    geom_ref,
    lift_raw,
    spread_ref,
    table,
    inner,
    gathered,
    hot_local,
    hot_ghost,
    hot_send,
    out_buf,
    ghost,
    load_sem,
    send_sem,
    recv_sem,
):
    loads = [
        pltpu.make_async_copy(src, dst, load_sem.at[i])
        for i, (src, dst) in enumerate(
            (
                (fields_hbm, adv_ref),
                (send_hbm, send_ref),
                (pick_hbm, pick_ref),
                (pack_hbm, pack_ref),
                (source_hbm, source_ref),
                (deriv_hbm, deriv_ref),
                (metric_hbm, metric_ref),
                (curved_hbm, curved_ref),
                (ratio_hbm, ratio_ref),
                (unpack_hbm, unpack_ref),
                (turn_hbm, turn_ref),
                (perm_hbm, perm_ref),
                (geom_hbm, geom_ref),
                (lift_hbm, lift_raw),
                (spread_hbm, spread_ref),
            )
        )
    ]
    for load in loads:
        load.start()
    elements = adv_ref.shape[2]
    faces = 4 * elements
    cap = send_ref.shape[2]
    slots = 3 * n_sub * cap
    g = lax.axis_index("dom")
    me = lax.axis_index("sub")
    below = g > 0
    above = g < n_dom - 1
    send_ok = (below, None, above)
    recv_ok = (above, None, below)

    def guarded(ok, act):
        if ok is None:
            act()
        else:
            pl.when(ok)(act)

    def peers(o):
        return [lax.rem(me + d, n_sub) for d in range(1 if o == 1 else 0, n_sub)]

    def rows(o, j):
        return pl.ds(pl.multiple_of((o * n_sub + j) * cap, cap), cap)

    barrier = pltpu.get_barrier_semaphore()
    for o in range(3):

        def greet(o=o):
            for j in peers(o):
                pl.semaphore_signal(barrier, inc=1, device_id=(g + o - 1, j), device_id_type=MESH)

        guarded(send_ok[o], greet)

    def copy(step, o, j):
        return pltpu.make_async_remote_copy(
            src_ref=out_buf.at[step, rows(o, j)],
            dst_ref=ghost.at[step, rows(o, me)],
            send_sem=send_sem.at[step, o, j],
            recv_sem=recv_sem.at[step, o, me],
            device_id=(g + o - 1, j),
            device_id_type=MESH,
        )

    def arrival(step, o, j):
        return pltpu.make_async_remote_copy(
            src_ref=out_buf.at[step, rows(o, j)],
            dst_ref=ghost.at[step, rows(o, j)],
            send_sem=send_sem.at[step, o, j],
            recv_sem=recv_sem.at[step, o, j],
            device_id=(g - o + 1, j),
            device_id_type=MESH,
        )

    loads[1].wait()
    square_r = lax.broadcasted_iota(jnp.int32, (cap, cap), 0)
    square_c = lax.broadcasted_iota(jnp.int32, (cap, cap), 1)
    face_lane = lax.broadcasted_iota(jnp.int32, (cap, faces), 1)
    for o in range(3):
        for j in range(n_sub):
            row = send_ref[o, j : j + 1, :]
            column = jnp.sum(jnp.where(square_r == square_c, row, 0), axis=1, keepdims=True)
            at = (o * n_sub + j) * cap
            hot_send[at : at + cap, :] = jnp.where(face_lane == column, 1.0, 0.0).astype(BF16)

    for load in (loads[0], loads[2], loads[3]):
        load.wait()
    alive = lax.broadcasted_iota(jnp.int32, (1, elements), 1) < live_ref[0]

    for step in range(2):
        parts = []
        for c in range(6):
            if step == 0:
                u = jnp.where(alive, adv_ref[c], 0.0)
                adv_ref[c] = u
            else:
                u = adv_ref[c]
            parts.append(halves(u))
        pick = pick_ref[...]
        for q in range(2):
            high = [dot(pick, parts[3 * q + c][0]) for c in range(3)]
            low = [dot(pick, parts[3 * q + c][1]) for c in range(3)]
            for f in range(4):
                at = f * ROWS
                h = jnp.concatenate([x[at : at + ROWS] for x in high], axis=0)
                l = jnp.concatenate([x[at : at + ROWS] for x in low], axis=0)
                inner[q, f] = h + l
                table[q * PAIR : (q + 1) * PAIR, f * elements : (f + 1) * elements] = jnp.concatenate(
                    [h, l], axis=0
                ).astype(BF16)
        outgoing = dot_nt(hot_send[...], table[...])
        out_buf[step] = dot(outgoing.astype(BF16), pack_ref[...])

        if step == 0:
            for k in range(2):

                def blank_above(k=k):
                    ghost[k, 0 : n_sub * cap, :] = jnp.zeros((n_sub * cap, LANES), F32)

                def blank_below(k=k):
                    ghost[k, 2 * n_sub * cap :, :] = jnp.zeros((n_sub * cap, LANES), F32)

                pl.when(jnp.logical_not(above))(blank_above)
                pl.when(jnp.logical_not(below))(blank_below)
            sides = jnp.minimum(g, 1) + jnp.minimum(n_dom - 1 - g, 1)
            pl.semaphore_wait(barrier, n_sub * (sides + 1) - 1)
        for o in (2, 0, 1):

            def start(o=o):
                for j in peers(o):
                    copy(step, o, j).start()

            guarded(send_ok[o], start)
        ghost[step, rows(1, me), :] = out_buf[step, rows(1, me), :]

        if step == 0:
            for load in loads[4:]:
                load.wait()
            local_row = lax.broadcasted_iota(jnp.int32, (faces, elements), 0)
            ghost_row = lax.broadcasted_iota(jnp.int32, (slots, elements), 0) + faces
            for f in range(4):
                source = source_ref[f : f + 1, :]
                lanes = slice(f * elements, (f + 1) * elements)
                hot_local[:, lanes] = jnp.where(local_row == source, 1.0, 0.0).astype(BF16)
                hot_ghost[:, lanes] = jnp.where(ghost_row == source, 1.0, 0.0).astype(BF16)
            ratio = jnp.where(curved_ref[...] == 1, ratio_ref[...], 1.0)
            scale[...] = jnp.where(alive, ratio, 0.0)
            deriv = deriv_ref[...].reshape(3 * NODES, NODES)
            deriv_high, deriv_low = halves(deriv)
            lift_parts = jnp.concatenate([x.astype(F32) for x in halves(lift_raw[...])], axis=0)
            lift_ref[...] = dot(lift_parts.astype(BF16), spread_ref[...]).astype(BF16)

        def slope(c):
            high, low = parts[c]
            s = dot(deriv_high, high) + (dot(deriv_low, high) + dot(deriv_high, low))
            return s[0:NODES], s[NODES : 2 * NODES], s[2 * NODES :]

        def along(s, x):
            return (
                metric_ref[x : x + 1, :] * s[0]
                + metric_ref[3 + x : 4 + x, :] * s[1]
                + metric_ref[6 + x : 7 + x, :] * s[2]
            )

        for q in range(2):
            sx, sy, sz = slope(3 * q), slope(3 * q + 1), slope(3 * q + 2)
            curl = (
                along(sz, 1) - along(sy, 2),
                along(sx, 2) - along(sz, 0),
                along(sy, 0) - along(sx, 1),
            )
            for c in range(3):
                if q == 0:
                    volume[3 + c] = curl[c]
                else:
                    volume[c] = -curl[c]
        for f in range(4):
            lanes = slice(f * elements, (f + 1) * elements)
            gathered[:, lanes] = dot(table[...], hot_local[:, lanes])

        for o in range(3):

            def land(o=o):
                for j in peers(o):
                    arrival(step, o, j).wait_recv()

            guarded(recv_ok[o], land)

        ghost_high, ghost_low = halves(ghost[step])
        far_high = dot_nt(unpack_ref[...], ghost_high)
        far_low = dot_nt(unpack_ref[...], ghost_low)
        far = jnp.concatenate(
            [far_high[:GROUP], far_low[:GROUP], far_high[GROUP:], far_low[GROUP:]], axis=0
        ).astype(BF16)

        turn = turn_ref[...]
        flux = [[] for _ in range(6)]
        for f in range(4):
            lanes = slice(f * elements, (f + 1) * elements)
            outer = gathered[:, lanes] + dot(far, hot_ghost[:, lanes])
            symmetry = perm_ref[f : f + 1, :]
            jump = []
            for q in range(2):
                pair = outer[q * PAIR : (q + 1) * PAIR]
                turned = dot(turn, pair.astype(BF16))
                exterior = pair[:GROUP] + pair[GROUP:]
                for p in range(1, 6):
                    exterior = jnp.where(symmetry == p, turned[(p - 1) * GROUP : p * GROUP], exterior)
                difference = exterior - inner[q, f]
                jump += [difference[c * ROWS : (c + 1) * ROWS] for c in range(3)]
            nx, ny, nz = (geom_ref[k, f : f + 1, :] for k in range(3))
            half = 0.5 * geom_ref[3, f : f + 1, :]
            along_h = nx * jump[0] + ny * jump[1] + nz * jump[2]
            along_e = nx * jump[3] + ny * jump[4] + nz * jump[5]
            flux[0].append(half * (nz * jump[4] - ny * jump[5] + jump[0] - along_h * nx))
            flux[1].append(half * (nx * jump[5] - nz * jump[3] + jump[1] - along_h * ny))
            flux[2].append(half * (ny * jump[3] - nx * jump[4] + jump[2] - along_h * nz))
            flux[3].append(half * (ny * jump[2] - nz * jump[1] + jump[3] - along_e * nx))
            flux[4].append(half * (nz * jump[0] - nx * jump[2] + jump[4] - along_e * ny))
            flux[5].append(half * (nx * jump[1] - ny * jump[0] + jump[5] - along_e * nz))
        for c in range(6):
            high, low = halves(jnp.concatenate(flux[c], axis=0))
            if step == 1:
                flux_high[c] = high
                flux_low[c] = low
            else:
                register = TIME_STEP * ((volume[c] + lifted(lift_ref[...], high, low)) * scale[...])
                reg_ref[c] = register
                adv_ref[c] = adv_ref[c] + RK_B[0] * register

    for step in range(2):
        for o in range(3):

            def sent(o=o, step=step):
                for j in peers(o):
                    copy(step, o, j).wait_send()

            guarded(send_ok[o], sent)


def finish(
    adv_ref, reg_ref, volume, scale, flux_high, flux_low, lift_ref, adv_hbm, reg_hbm, adv_out, reg_out, sem
):
    writes = []
    for c in range(6):
        register = TIME_STEP * ((volume[c] + lifted(lift_ref[...], flux_high[c], flux_low[c])) * scale[...])
        register = RK_A[1] * reg_ref[c] + register
        reg_out[c] = register
        adv_out[c] = adv_ref[c] + RK_B[1] * register
        for k, (src, dst) in enumerate(((reg_out, reg_hbm), (adv_out, adv_hbm))):
            write = pltpu.make_async_copy(src.at[c], dst.at[c], sem.at[k, c])
            write.start()
            writes.append(write)
    for write in writes:
        write.wait()


def on_device(
    n_dom,
    n_sub,
    fields,
    metric,
    face_geom,
    jacobian_ratio,
    curved,
    derivatives,
    lift_matrix,
    live_count,
    send_list,
    face_source,
    face_permutation,
):
    elements = fields.shape[2]
    faces = 4 * elements
    slots = 3 * n_sub * send_list.shape[3]
    vmem = pl.BlockSpec(memory_space=pltpu.VMEM)
    hbm = pl.BlockSpec(memory_space=pltpu.HBM)
    pick, spread, turn, pack, unpack = zero_one_matrices()
    operands = (
        fields,
        send_list.reshape(send_list.shape[1:]),
        pick,
        pack,
        face_source,
        derivatives,
        metric,
        curved.reshape(1, elements),
        jacobian_ratio,
        unpack,
        turn,
        face_permutation,
        face_geom,
        lift_matrix,
        spread,
    )
    operands = [pltpu.with_memory_space_constraint(a, pltpu.HBM) for a in operands]
    held = [pltpu.VMEM(a.shape, a.dtype) for a in operands[1:]]
    whole = jax.ShapeDtypeStruct(fields.shape, F32)
    flux = jax.ShapeDtypeStruct((6, 4 * ROWS, elements), BF16)
    carried = pl.pallas_call(
        functools.partial(kernel, n_dom, n_sub),
        out_shape=(
            whole,
            whole,
            whole,
            jax.ShapeDtypeStruct((NODES, elements), F32),
            flux,
            flux,
            jax.ShapeDtypeStruct((2 * NODES, 4 * ROWS), BF16),
        ),
        in_specs=[pl.BlockSpec(memory_space=pltpu.SMEM)] + [hbm] * 15,
        out_specs=(vmem,) * 7,
        scratch_shapes=held
        + [
            pltpu.VMEM((2 * PAIR, faces), BF16),
            pltpu.VMEM((2, 4, GROUP, elements), F32),
            pltpu.VMEM((2 * PAIR, faces), F32),
            pltpu.VMEM((faces, faces), BF16),
            pltpu.VMEM((slots, faces), BF16),
            pltpu.VMEM((slots, faces), BF16),
            pltpu.VMEM((2, slots, LANES), F32),
            pltpu.VMEM((2, slots, LANES), F32),
            pltpu.SemaphoreType.DMA((15,)),
            pltpu.SemaphoreType.DMA((2, 3, n_sub)),
            pltpu.SemaphoreType.DMA((2, 3, n_sub)),
        ],
        compiler_params=pltpu.CompilerParams(
            collective_id=0, has_side_effects=True, vmem_limit_bytes=40 * 1024 * 1024
        ),
        cost_estimate=pl.CostEstimate(flops=4_000_000_000, bytes_accessed=2_000_000, transcendentals=0),
    )(live_count, *operands)
    return pl.pallas_call(
        finish,
        out_shape=(whole, whole),
        in_specs=[vmem] * 7,
        out_specs=(hbm, hbm),
        scratch_shapes=[
            pltpu.VMEM(fields.shape, F32),
            pltpu.VMEM(fields.shape, F32),
            pltpu.SemaphoreType.DMA((2, 6)),
        ],
        compiler_params=pltpu.CompilerParams(vmem_limit_bytes=40 * 1024 * 1024),
        cost_estimate=pl.CostEstimate(flops=100_000_000, bytes_accessed=2_000_000, transcendentals=0),
    )(*carried)


def solution(mesh):
    return jax.shard_map(
        functools.partial(on_device, mesh.shape["dom"], mesh.shape["sub"]),
        mesh=mesh,
        in_specs=(
            P(None, None, ("dom", "sub")),
            P(None, ("dom", "sub")),
            P(None, None, ("dom", "sub")),
            P(None, ("dom", "sub")),
            P(("dom", "sub")),
            P(),
            P(),
            P(("dom", "sub")),
            P(("dom", "sub"), None, None, None),
            P(None, ("dom", "sub")),
            P(None, ("dom", "sub")),
        ),
        out_specs=(P(None, None, ("dom", "sub")), P(None, None, ("dom", "sub"))),
        check_vma=False,
    )
```

```python
import functools

import jax
import jax.numpy as jnp
import numpy as np
from jax import lax
from jax.experimental import pallas as pl
from jax.experimental.pallas import tpu as pltpu
from jax.sharding import PartitionSpec as P

RK_A = (0.0, -567301805773.0 / 1357537059087.0)
RK_B = (1432997174477.0 / 9575080441755.0, 5161836677717.0 / 13612068292357.0)
TIME_STEP = 0.5
SYMMETRIES = ((0, 1, 2), (1, 2, 0), (2, 0, 1), (0, 2, 1), (2, 1, 0), (1, 0, 2))
F32 = jnp.float32
BF16 = jnp.bfloat16
NODES = 56
TRACE = 21
ROWS = 24
GROUP = 3 * ROWS
PAIR = 2 * GROUP
LANES = 128
MESH = pl.DeviceIdType.MESH


def node_tables():
    volume_nodes = [(i, j, k) for i in range(6) for j in range(6 - i) for k in range(6 - i - j)]
    volume_index = {v: n for n, v in enumerate(volume_nodes)}
    triangle = [(a, b) for a in range(6) for b in range(6 - a)]
    triangle_index = {t: n for n, t in enumerate(triangle)}
    face_nodes = np.array(
        [
            [volume_index[a, b, 0] for a, b in triangle],
            [volume_index[a, 0, b] for a, b in triangle],
            [volume_index[a, b, 5 - a - b] for a, b in triangle],
            [volume_index[0, a, b] for a, b in triangle],
        ],
        np.int32,
    )
    permuted = np.array(
        [
            [triangle_index[(a, b, 5 - a - b)[q[0]], (a, b, 5 - a - b)[q[1]]] for a, b in triangle]
            for q in SYMMETRIES
        ],
        np.int32,
    )
    return (face_nodes, permuted)


def zero_one_matrices():
    face_nodes, permuted = node_tables()
    pick = np.zeros((4 * ROWS, NODES), np.float32)
    spread = np.zeros((4 * TRACE, 4 * ROWS), np.float32)
    for f in range(4):
        for m in range(TRACE):
            pick[f * ROWS + m, face_nodes[f, m]] = 1
            spread[f * TRACE + m, f * ROWS + m] = 1
    turn = np.zeros((5 * GROUP, PAIR), np.float32)
    for p in range(1, 6):
        for c in range(3):
            for m in range(TRACE):
                for part in range(2):
                    turn[(p - 1) * GROUP + c * ROWS + m, part * GROUP + c * ROWS + permuted[p, m]] = 1
    pack = np.zeros((LANES, 2 * PAIR), np.float32)
    unpack = np.zeros((2 * GROUP, LANES), np.float32)
    for q in range(2):
        for c in range(3):
            for m in range(TRACE):
                lane = (3 * q + c) * TRACE + m
                unpack[q * GROUP + c * ROWS + m, lane] = 1
                for part in range(2):
                    pack[lane, q * PAIR + part * GROUP + c * ROWS + m] = 1
    return tuple(jnp.asarray(a, BF16) for a in (pick, spread, turn, pack, unpack))


def halves(x):
    high = x.astype(BF16)
    low = (x - high.astype(F32)).astype(BF16)
    return high, low


def dot(a, b):
    return jnp.dot(a, b, preferred_element_type=F32)


def dot_nt(a, b):
    return lax.dot_general(a, b, (((1,), (1,)), ((), ())), preferred_element_type=F32)


def lifted(lift, high, low):
    main = dot(lift, high)
    return main[:NODES] + (main[NODES:] + dot(lift, low)[:NODES])


def kernel(
    n_dom,
    n_sub,
    live_ref,
    fields_hbm,
    send_hbm,
    pick_hbm,
    pack_hbm,
    source_hbm,
    deriv_hbm,
    metric_hbm,
    curved_hbm,
    ratio_hbm,
    unpack_hbm,
    turn_hbm,
    perm_hbm,
    geom_hbm,
    lift_hbm,
    spread_hbm,
    adv_ref,
    reg_ref,
    volume,
    scale,
    flux_high,
    flux_low,
    lift_ref,
    send_ref,
    pick_ref,
    pack_ref,
    source_ref,
    deriv_ref,
    metric_ref,
    curved_ref,
    ratio_ref,
    unpack_ref,
    turn_ref,
    perm_ref,
    geom_ref,
    lift_raw,
    spread_ref,
    table,
    inner,
    gathered,
    hot_local,
    hot_ghost,
    hot_send,
    send_row,
    out_buf,
    ghost,
    load_sem,
    send_sem,
    recv_sem,
):
    loads = [
        pltpu.make_async_copy(src, dst, load_sem.at[i])
        for i, (src, dst) in enumerate(
            (
                (fields_hbm, adv_ref),
                (send_hbm, send_ref),
                (pick_hbm, pick_ref),
                (pack_hbm, pack_ref),
                (source_hbm, source_ref),
                (deriv_hbm, deriv_ref),
                (metric_hbm, metric_ref),
                (curved_hbm, curved_ref),
                (ratio_hbm, ratio_ref),
                (unpack_hbm, unpack_ref),
                (turn_hbm, turn_ref),
                (perm_hbm, perm_ref),
                (geom_hbm, geom_ref),
                (lift_hbm, lift_raw),
                (spread_hbm, spread_ref),
            )
        )
    ]
    for i in (1, 0, 2, 3, *range(4, len(loads))):
        loads[i].start()
    elements = adv_ref.shape[2]
    faces = 4 * elements
    cap = send_ref.shape[2]
    slots = 3 * n_sub * cap
    g = lax.axis_index("dom")
    me = lax.axis_index("sub")
    below = g > 0
    above = g < n_dom - 1
    send_ok = (below, None, above)
    recv_ok = (above, None, below)

    def guarded(ok, act):
        if ok is None:
            act()
        else:
            pl.when(ok)(act)

    def peers(o):
        return [lax.rem(me + d, n_sub) for d in range(1 if o == 1 else 0, n_sub)]

    def rows(o, j):
        return pl.ds(pl.multiple_of((o * n_sub + j) * cap, cap), cap)

    barrier = pltpu.get_barrier_semaphore()
    for o in range(3):

        def greet(o=o):
            for j in peers(o):
                pl.semaphore_signal(barrier, inc=1, device_id=(g + o - 1, j), device_id_type=MESH)

        guarded(send_ok[o], greet)

    def copy(step, o, j):
        return pltpu.make_async_remote_copy(
            src_ref=out_buf.at[step, rows(o, j)],
            dst_ref=ghost.at[step, rows(o, me)],
            send_sem=send_sem.at[step, o, j],
            recv_sem=recv_sem.at[step, o, me],
            device_id=(g + o - 1, j),
            device_id_type=MESH,
        )

    def arrival(step, o, j):
        return pltpu.make_async_remote_copy(
            src_ref=out_buf.at[step, rows(o, j)],
            dst_ref=ghost.at[step, rows(o, j)],
            send_sem=send_sem.at[step, o, j],
            recv_sem=recv_sem.at[step, o, j],
            device_id=(g - o + 1, j),
            device_id_type=MESH,
        )

    loads[1].wait()
    send_row[...] = jnp.full(send_row.shape, -1, jnp.int32)
    for o in range(3):
        for j in range(n_sub):
            at = (o * n_sub + j) * cap
            send_row[:, at : at + cap] = send_ref[o, j : j + 1, :]
    face_row = lax.broadcasted_iota(jnp.int32, hot_send.shape, 0)
    hot_send[...] = jnp.where(face_row == send_row[...], 1.0, 0.0).astype(BF16)
    for load in (loads[0], loads[2], loads[3]):
        load.wait()
    alive = lax.broadcasted_iota(jnp.int32, (1, elements), 1) < live_ref[0]

    for step in range(2):
        parts = []
        for c in range(6):
            if step == 0:
                u = jnp.where(alive, adv_ref[c], 0.0)
                adv_ref[c] = u
            else:
                u = adv_ref[c]
            parts.append(halves(u))
        pick = pick_ref[...]
        for q in range(2):
            high = [dot(pick, parts[3 * q + c][0]) for c in range(3)]
            low = [dot(pick, parts[3 * q + c][1]) for c in range(3)]
            for f in range(4):
                at = f * ROWS
                h = jnp.concatenate([x[at : at + ROWS] for x in high], axis=0)
                l = jnp.concatenate([x[at : at + ROWS] for x in low], axis=0)
                inner[q, f] = h + l
                table[q * PAIR : (q + 1) * PAIR, f * elements : (f + 1) * elements] = jnp.concatenate(
                    [h, l], axis=0
                ).astype(BF16)
        outgoing = dot(table[...], hot_send[...])
        out_buf[step] = dot(pack_ref[...], outgoing.astype(BF16)).T

        if step == 0:
            for k in range(2):

                def blank_above(k=k):
                    ghost[k, 0 : n_sub * cap, :] = jnp.zeros((n_sub * cap, LANES), F32)

                def blank_below(k=k):
                    ghost[k, 2 * n_sub * cap :, :] = jnp.zeros((n_sub * cap, LANES), F32)

                pl.when(jnp.logical_not(above))(blank_above)
                pl.when(jnp.logical_not(below))(blank_below)
            sides = jnp.minimum(g, 1) + jnp.minimum(n_dom - 1 - g, 1)
            pl.semaphore_wait(barrier, n_sub * (sides + 1) - 1)
        for o in (2, 0, 1):

            def start(o=o):
                for j in peers(o):
                    copy(step, o, j).start()

            guarded(send_ok[o], start)
        ghost[step, rows(1, me), :] = out_buf[step, rows(1, me), :]

        if step == 0:
            for load in loads[4:]:
                load.wait()
            local_row = lax.broadcasted_iota(jnp.int32, (faces, elements), 0)
            ghost_row = lax.broadcasted_iota(jnp.int32, (slots, elements), 0) + faces
            for f in range(4):
                source = source_ref[f : f + 1, :]
                lanes = slice(f * elements, (f + 1) * elements)
                hot_local[:, lanes] = jnp.where(local_row == source, 1.0, 0.0).astype(BF16)
                hot_ghost[:, lanes] = jnp.where(ghost_row == source, 1.0, 0.0).astype(BF16)
            ratio = jnp.where(curved_ref[...] == 1, ratio_ref[...], 1.0)
            scale[...] = jnp.where(alive, ratio, 0.0)
            deriv = deriv_ref[...].reshape(3 * NODES, NODES)
            deriv_high, deriv_low = halves(deriv)
            lift_parts = jnp.concatenate([x.astype(F32) for x in halves(lift_raw[...])], axis=0)
            lift_ref[...] = dot(lift_parts.astype(BF16), spread_ref[...]).astype(BF16)

        def slope(c):
            high, low = parts[c]
            s = dot(deriv_high, high) + (dot(deriv_low, high) + dot(deriv_high, low))
            return s[0:NODES], s[NODES : 2 * NODES], s[2 * NODES :]

        def along(s, x):
            return (
                metric_ref[x : x + 1, :] * s[0]
                + metric_ref[3 + x : 4 + x, :] * s[1]
                + metric_ref[6 + x : 7 + x, :] * s[2]
            )

        for q in range(2):
            sx, sy, sz = slope(3 * q), slope(3 * q + 1), slope(3 * q + 2)
            curl = (
                along(sz, 1) - along(sy, 2),
                along(sx, 2) - along(sz, 0),
                along(sy, 0) - along(sx, 1),
            )
            for c in range(3):
                if q == 0:
                    volume[3 + c] = curl[c]
                else:
                    volume[c] = -curl[c]
        for f in range(4):
            lanes = slice(f * elements, (f + 1) * elements)
            gathered[:, lanes] = dot(table[...], hot_local[:, lanes])

        for o in range(3):

            def land(o=o):
                for j in peers(o):
                    arrival(step, o, j).wait_recv()

            guarded(recv_ok[o], land)

        ghost_high, ghost_low = halves(ghost[step])
        far_high = dot_nt(unpack_ref[...], ghost_high)
        far_low = dot_nt(unpack_ref[...], ghost_low)
        far = jnp.concatenate(
            [far_high[:GROUP], far_low[:GROUP], far_high[GROUP:], far_low[GROUP:]], axis=0
        ).astype(BF16)

        turn = turn_ref[...]
        flux = [[] for _ in range(6)]
        for f in range(4):
            lanes = slice(f * elements, (f + 1) * elements)
            outer = gathered[:, lanes] + dot(far, hot_ghost[:, lanes])
            symmetry = perm_ref[f : f + 1, :]
            jump = []
            for q in range(2):
                pair = outer[q * PAIR : (q + 1) * PAIR]
                turned = dot(turn, pair.astype(BF16))
                exterior = pair[:GROUP] + pair[GROUP:]
                for p in range(1, 6):
                    exterior = jnp.where(symmetry == p, turned[(p - 1) * GROUP : p * GROUP], exterior)
                difference = exterior - inner[q, f]
                jump += [difference[c * ROWS : (c + 1) * ROWS] for c in range(3)]
            nx, ny, nz = (geom_ref[k, f : f + 1, :] for k in range(3))
            half = 0.5 * geom_ref[3, f : f + 1, :]
            along_h = nx * jump[0] + ny * jump[1] + nz * jump[2]
            along_e = nx * jump[3] + ny * jump[4] + nz * jump[5]
            flux[0].append(half * (nz * jump[4] - ny * jump[5] + jump[0] - along_h * nx))
            flux[1].append(half * (nx * jump[5] - nz * jump[3] + jump[1] - along_h * ny))
            flux[2].append(half * (ny * jump[3] - nx * jump[4] + jump[2] - along_h * nz))
            flux[3].append(half * (ny * jump[2] - nz * jump[1] + jump[3] - along_e * nx))
            flux[4].append(half * (nz * jump[0] - nx * jump[2] + jump[4] - along_e * ny))
            flux[5].append(half * (nx * jump[1] - ny * jump[0] + jump[5] - along_e * nz))
        for c in range(6):
            high, low = halves(jnp.concatenate(flux[c], axis=0))
            if step == 1:
                flux_high[c] = high
                flux_low[c] = low
            else:
                register = TIME_STEP * ((volume[c] + lifted(lift_ref[...], high, low)) * scale[...])
                reg_ref[c] = register
                adv_ref[c] = adv_ref[c] + RK_B[0] * register

    for step in range(2):
        for o in range(3):

            def sent(o=o, step=step):
                for j in peers(o):
                    copy(step, o, j).wait_send()

            guarded(send_ok[o], sent)


def finish(
    adv_ref, reg_ref, volume, scale, flux_high, flux_low, lift_ref, adv_hbm, reg_hbm, adv_out, reg_out, sem
):
    writes = []
    for c in range(6):
        register = TIME_STEP * ((volume[c] + lifted(lift_ref[...], flux_high[c], flux_low[c])) * scale[...])
        register = RK_A[1] * reg_ref[c] + register
        reg_out[c] = register
        adv_out[c] = adv_ref[c] + RK_B[1] * register
        for k, (src, dst) in enumerate(((reg_out, reg_hbm), (adv_out, adv_hbm))):
            write = pltpu.make_async_copy(src.at[c], dst.at[c], sem.at[k, c])
            write.start()
            writes.append(write)
    for write in writes:
        write.wait()


def on_device(
    n_dom,
    n_sub,
    fields,
    metric,
    face_geom,
    jacobian_ratio,
    curved,
    derivatives,
    lift_matrix,
    live_count,
    send_list,
    face_source,
    face_permutation,
):
    elements = fields.shape[2]
    faces = 4 * elements
    slots = 3 * n_sub * send_list.shape[3]
    slot_lanes = -(-slots // LANES) * LANES
    vmem = pl.BlockSpec(memory_space=pltpu.VMEM)
    hbm = pl.BlockSpec(memory_space=pltpu.HBM)
    pick, spread, turn, pack, unpack = zero_one_matrices()
    operands = (
        fields,
        send_list.reshape(send_list.shape[1:]),
        pick,
        pack,
        face_source,
        derivatives,
        metric,
        curved.reshape(1, elements),
        jacobian_ratio,
        unpack,
        turn,
        face_permutation,
        face_geom,
        lift_matrix,
        spread,
    )
    operands = [pltpu.with_memory_space_constraint(a, pltpu.HBM) for a in operands]
    held = [pltpu.VMEM(a.shape, a.dtype) for a in operands[1:]]
    whole = jax.ShapeDtypeStruct(fields.shape, F32)
    flux = jax.ShapeDtypeStruct((6, 4 * ROWS, elements), BF16)
    carried = pl.pallas_call(
        functools.partial(kernel, n_dom, n_sub),
        out_shape=(
            whole,
            whole,
            whole,
            jax.ShapeDtypeStruct((NODES, elements), F32),
            flux,
            flux,
            jax.ShapeDtypeStruct((2 * NODES, 4 * ROWS), BF16),
        ),
        in_specs=[pl.BlockSpec(memory_space=pltpu.SMEM)] + [hbm] * 15,
        out_specs=(vmem,) * 7,
        scratch_shapes=held
        + [
            pltpu.VMEM((2 * PAIR, faces), BF16),
            pltpu.VMEM((2, 4, GROUP, elements), F32),
            pltpu.VMEM((2 * PAIR, faces), F32),
            pltpu.VMEM((faces, faces), BF16),
            pltpu.VMEM((slots, faces), BF16),
            pltpu.VMEM((faces, slot_lanes), BF16),
            pltpu.VMEM((1, slot_lanes), jnp.int32),
            pltpu.VMEM((2, slot_lanes, LANES), F32),
            pltpu.VMEM((2, slots, LANES), F32),
            pltpu.SemaphoreType.DMA((15,)),
            pltpu.SemaphoreType.DMA((2, 3, n_sub)),
            pltpu.SemaphoreType.DMA((2, 3, n_sub)),
        ],
        compiler_params=pltpu.CompilerParams(
            collective_id=0, has_side_effects=True, vmem_limit_bytes=40 * 1024 * 1024
        ),
        cost_estimate=pl.CostEstimate(flops=4_000_000_000, bytes_accessed=2_000_000, transcendentals=0),
    )(live_count, *operands)
    return pl.pallas_call(
        finish,
        out_shape=(whole, whole),
        in_specs=[vmem] * 7,
        out_specs=(hbm, hbm),
        scratch_shapes=[
            pltpu.VMEM(fields.shape, F32),
            pltpu.VMEM(fields.shape, F32),
            pltpu.SemaphoreType.DMA((2, 6)),
        ],
        compiler_params=pltpu.CompilerParams(vmem_limit_bytes=40 * 1024 * 1024),
        cost_estimate=pl.CostEstimate(flops=100_000_000, bytes_accessed=2_000_000, transcendentals=0),
    )(*carried)


def solution(mesh):
    return jax.shard_map(
        functools.partial(on_device, mesh.shape["dom"], mesh.shape["sub"]),
        mesh=mesh,
        in_specs=(
            P(None, None, ("dom", "sub")),
            P(None, ("dom", "sub")),
            P(None, None, ("dom", "sub")),
            P(None, ("dom", "sub")),
            P(("dom", "sub")),
            P(),
            P(),
            P(("dom", "sub")),
            P(("dom", "sub"), None, None, None),
            P(None, ("dom", "sub")),
            P(None, ("dom", "sub")),
        ),
        out_specs=(P(None, None, ("dom", "sub")), P(None, None, ("dom", "sub"))),
        check_vma=False,
    )
```

```python
import functools

import jax
import jax.numpy as jnp
import numpy as np
from jax import lax
from jax.experimental import pallas as pl
from jax.experimental.pallas import tpu as pltpu
from jax.sharding import PartitionSpec as P

RK_A = (0.0, -567301805773.0 / 1357537059087.0)
RK_B = (1432997174477.0 / 9575080441755.0, 5161836677717.0 / 13612068292357.0)
TIME_STEP = 0.5
SYMMETRIES = ((0, 1, 2), (1, 2, 0), (2, 0, 1), (0, 2, 1), (2, 1, 0), (1, 0, 2))
F32 = jnp.float32
BF16 = jnp.bfloat16
NODES = 56
TRACE = 21
ROWS = 24
GROUP = 3 * ROWS
PAIR = 2 * GROUP
LANES = 128
MESH = pl.DeviceIdType.MESH


def node_tables():
    volume_nodes = [(i, j, k) for i in range(6) for j in range(6 - i) for k in range(6 - i - j)]
    volume_index = {v: n for n, v in enumerate(volume_nodes)}
    triangle = [(a, b) for a in range(6) for b in range(6 - a)]
    triangle_index = {t: n for n, t in enumerate(triangle)}
    face_nodes = np.array(
        [
            [volume_index[a, b, 0] for a, b in triangle],
            [volume_index[a, 0, b] for a, b in triangle],
            [volume_index[a, b, 5 - a - b] for a, b in triangle],
            [volume_index[0, a, b] for a, b in triangle],
        ],
        np.int32,
    )
    permuted = np.array(
        [
            [triangle_index[(a, b, 5 - a - b)[q[0]], (a, b, 5 - a - b)[q[1]]] for a, b in triangle]
            for q in SYMMETRIES
        ],
        np.int32,
    )
    return (face_nodes, permuted)


def zero_one_matrices():
    face_nodes, permuted = node_tables()
    pick = np.zeros((4 * ROWS, NODES), np.float32)
    spread = np.zeros((4 * TRACE, 4 * ROWS), np.float32)
    for f in range(4):
        for m in range(TRACE):
            pick[f * ROWS + m, face_nodes[f, m]] = 1
            spread[f * TRACE + m, f * ROWS + m] = 1
    turn = np.zeros((5 * GROUP, PAIR), np.float32)
    for p in range(1, 6):
        for c in range(3):
            for m in range(TRACE):
                for part in range(2):
                    turn[(p - 1) * GROUP + c * ROWS + m, part * GROUP + c * ROWS + permuted[p, m]] = 1
    pack = np.zeros((2 * PAIR, LANES), np.float32)
    unpack = np.zeros((2 * GROUP, LANES), np.float32)
    for q in range(2):
        for c in range(3):
            for m in range(TRACE):
                lane = (3 * q + c) * TRACE + m
                unpack[q * GROUP + c * ROWS + m, lane] = 1
                for part in range(2):
                    pack[q * PAIR + part * GROUP + c * ROWS + m, lane] = 1
    return tuple(jnp.asarray(a, BF16) for a in (pick, spread, turn, pack, unpack))


def halves(x):
    high = x.astype(BF16)
    low = (x - high.astype(F32)).astype(BF16)
    return high, low


def dot(a, b):
    return jnp.dot(a, b, preferred_element_type=F32)


def dot_nt(a, b):
    return lax.dot_general(a, b, (((1,), (1,)), ((), ())), preferred_element_type=F32)


def lifted(lift, high, low):
    main = dot(lift, high)
    return main[:NODES] + (main[NODES:] + dot(lift, low)[:NODES])


def kernel(
    n_dom,
    n_sub,
    live_ref,
    fields_hbm,
    send_hbm,
    pick_hbm,
    pack_hbm,
    source_hbm,
    deriv_hbm,
    metric_hbm,
    curved_hbm,
    ratio_hbm,
    unpack_hbm,
    turn_hbm,
    perm_hbm,
    geom_hbm,
    lift_hbm,
    spread_hbm,
    adv_ref,
    reg_ref,
    volume,
    scale,
    flux_high,
    flux_low,
    lift_ref,
    send_ref,
    pick_ref,
    pack_ref,
    source_ref,
    deriv_ref,
    metric_ref,
    curved_ref,
    ratio_ref,
    unpack_ref,
    turn_ref,
    perm_ref,
    geom_ref,
    lift_raw,
    spread_ref,
    table,
    inner,
    gathered,
    hot_local,
    hot_ghost,
    hot_send,
    out_buf,
    ghost,
    load_sem,
    send_sem,
    recv_sem,
):
    loads = [
        pltpu.make_async_copy(src, dst, load_sem.at[i])
        for i, (src, dst) in enumerate(
            (
                (fields_hbm, adv_ref),
                (send_hbm, send_ref),
                (pick_hbm, pick_ref),
                (pack_hbm, pack_ref),
                (source_hbm, source_ref),
                (deriv_hbm, deriv_ref),
                (metric_hbm, metric_ref),
                (curved_hbm, curved_ref),
                (ratio_hbm, ratio_ref),
                (unpack_hbm, unpack_ref),
                (turn_hbm, turn_ref),
                (perm_hbm, perm_ref),
                (geom_hbm, geom_ref),
                (lift_hbm, lift_raw),
                (spread_hbm, spread_ref),
            )
        )
    ]
    for i in (1, 4, 0, 2, 3, *range(5, len(loads))):
        loads[i].start()
    elements = adv_ref.shape[2]
    faces = 4 * elements
    cap = send_ref.shape[2]
    slots = 3 * n_sub * cap
    g = lax.axis_index("dom")
    me = lax.axis_index("sub")
    below = g > 0
    above = g < n_dom - 1
    send_ok = (below, None, above)
    recv_ok = (above, None, below)

    def guarded(ok, act):
        if ok is None:
            act()
        else:
            pl.when(ok)(act)

    def peers(o):
        return [lax.rem(me + d, n_sub) for d in range(1 if o == 1 else 0, n_sub)]

    def rows(o, j):
        return pl.ds(pl.multiple_of((o * n_sub + j) * cap, cap), cap)

    barrier = pltpu.get_barrier_semaphore()
    for o in range(3):

        def greet(o=o):
            for j in peers(o):
                pl.semaphore_signal(barrier, inc=1, device_id=(g + o - 1, j), device_id_type=MESH)

        guarded(send_ok[o], greet)

    def copy(step, o, j):
        return pltpu.make_async_remote_copy(
            src_ref=out_buf.at[step, rows(o, j)],
            dst_ref=ghost.at[step, rows(o, me)],
            send_sem=send_sem.at[step, o, j],
            recv_sem=recv_sem.at[step, o, me],
            device_id=(g + o - 1, j),
            device_id_type=MESH,
        )

    def arrival(step, o, j):
        return pltpu.make_async_remote_copy(
            src_ref=out_buf.at[step, rows(o, j)],
            dst_ref=ghost.at[step, rows(o, j)],
            send_sem=send_sem.at[step, o, j],
            recv_sem=recv_sem.at[step, o, j],
            device_id=(g - o + 1, j),
            device_id_type=MESH,
        )

    loads[1].wait()
    square_r = lax.broadcasted_iota(jnp.int32, (cap, cap), 0)
    square_c = lax.broadcasted_iota(jnp.int32, (cap, cap), 1)
    face_lane = lax.broadcasted_iota(jnp.int32, (cap, faces), 1)
    for o in range(3):
        for j in range(n_sub):
            row = send_ref[o, j : j + 1, :]
            column = jnp.sum(jnp.where(square_r == square_c, row, 0), axis=1, keepdims=True)
            at = (o * n_sub + j) * cap
            hot_send[at : at + cap, :] = jnp.where(face_lane == column, 1.0, 0.0).astype(BF16)

    loads[4].wait()
    local_row = lax.broadcasted_iota(jnp.int32, (faces, elements), 0)
    ghost_row = lax.broadcasted_iota(jnp.int32, (slots, elements), 0) + faces
    for f in range(4):
        source = source_ref[f : f + 1, :]
        lanes = slice(f * elements, (f + 1) * elements)
        hot_local[:, lanes] = jnp.where(local_row == source, 1.0, 0.0).astype(BF16)
        hot_ghost[:, lanes] = jnp.where(ghost_row == source, 1.0, 0.0).astype(BF16)
    for load in (loads[0], loads[2], loads[3]):
        load.wait()
    alive = lax.broadcasted_iota(jnp.int32, (1, elements), 1) < live_ref[0]

    for step in range(2):
        parts = []
        for c in range(6):
            if step == 0:
                u = jnp.where(alive, adv_ref[c], 0.0)
                adv_ref[c] = u
            else:
                u = adv_ref[c]
            parts.append(halves(u))
        pick = pick_ref[...]
        for q in range(2):
            high = [dot(pick, parts[3 * q + c][0]) for c in range(3)]
            low = [dot(pick, parts[3 * q + c][1]) for c in range(3)]
            for f in range(4):
                at = f * ROWS
                h = jnp.concatenate([x[at : at + ROWS] for x in high], axis=0)
                l = jnp.concatenate([x[at : at + ROWS] for x in low], axis=0)
                inner[q, f] = h + l
                table[q * PAIR : (q + 1) * PAIR, f * elements : (f + 1) * elements] = jnp.concatenate(
                    [h, l], axis=0
                ).astype(BF16)
        outgoing = dot_nt(hot_send[...], table[...])
        out_buf[step] = dot(outgoing.astype(BF16), pack_ref[...])

        if step == 0:
            for k in range(2):

                def blank_above(k=k):
                    ghost[k, 0 : n_sub * cap, :] = jnp.zeros((n_sub * cap, LANES), F32)

                def blank_below(k=k):
                    ghost[k, 2 * n_sub * cap :, :] = jnp.zeros((n_sub * cap, LANES), F32)

                pl.when(jnp.logical_not(above))(blank_above)
                pl.when(jnp.logical_not(below))(blank_below)
            sides = jnp.minimum(g, 1) + jnp.minimum(n_dom - 1 - g, 1)
            pl.semaphore_wait(barrier, n_sub * (sides + 1) - 1)
        for o in (2, 0, 1):

            def start(o=o):
                for j in peers(o):
                    copy(step, o, j).start()

            guarded(send_ok[o], start)
        ghost[step, rows(1, me), :] = out_buf[step, rows(1, me), :]

        if step == 0:
            for load in loads[5:]:
                load.wait()
            ratio = jnp.where(curved_ref[...] == 1, ratio_ref[...], 1.0)
            scale[...] = jnp.where(alive, ratio, 0.0)
            deriv = deriv_ref[...].reshape(3 * NODES, NODES)
            deriv_high, deriv_low = halves(deriv)
            deriv_parts = jnp.concatenate(
                [deriv_high.astype(F32), deriv_low.astype(F32)], axis=0
            ).astype(BF16)
            lift_parts = jnp.concatenate([x.astype(F32) for x in halves(lift_raw[...])], axis=0)
            lift_ref[...] = dot(lift_parts.astype(BF16), spread_ref[...]).astype(BF16)

        def slope(c):
            high, low = parts[c]
            main = dot(deriv_parts, high)
            s = main[: 3 * NODES] + (main[3 * NODES :] + dot(deriv_high, low))
            return s[0:NODES], s[NODES : 2 * NODES], s[2 * NODES :]

        def along(s, x):
            return (
                metric_ref[x : x + 1, :] * s[0]
                + metric_ref[3 + x : 4 + x, :] * s[1]
                + metric_ref[6 + x : 7 + x, :] * s[2]
            )

        for q in range(2):
            sx, sy, sz = slope(3 * q), slope(3 * q + 1), slope(3 * q + 2)
            curl = (
                along(sz, 1) - along(sy, 2),
                along(sx, 2) - along(sz, 0),
                along(sy, 0) - along(sx, 1),
            )
            for c in range(3):
                if q == 0:
                    volume[3 + c] = curl[c]
                else:
                    volume[c] = -curl[c]
        for f in range(4):
            lanes = slice(f * elements, (f + 1) * elements)
            gathered[:, lanes] = dot(table[...], hot_local[:, lanes])

        for o in range(3):

            def land(o=o):
                for j in peers(o):
                    arrival(step, o, j).wait_recv()

            guarded(recv_ok[o], land)

        ghost_high, ghost_low = halves(ghost[step])
        far_high = dot_nt(unpack_ref[...], ghost_high)
        far_low = dot_nt(unpack_ref[...], ghost_low)
        far = jnp.concatenate(
            [far_high[:GROUP], far_low[:GROUP], far_high[GROUP:], far_low[GROUP:]], axis=0
        ).astype(BF16)

        turn = turn_ref[...]
        flux = [[] for _ in range(6)]
        for f in range(4):
            lanes = slice(f * elements, (f + 1) * elements)
            outer = gathered[:, lanes] + dot(far, hot_ghost[:, lanes])
            symmetry = perm_ref[f : f + 1, :]
            jump = []
            for q in range(2):
                pair = outer[q * PAIR : (q + 1) * PAIR]
                turned = dot(turn, pair.astype(BF16))
                exterior = pair[:GROUP] + pair[GROUP:]
                for p in range(1, 6):
                    exterior = jnp.where(symmetry == p, turned[(p - 1) * GROUP : p * GROUP], exterior)
                difference = exterior - inner[q, f]
                jump += [difference[c * ROWS : (c + 1) * ROWS] for c in range(3)]
            nx, ny, nz = (geom_ref[k, f : f + 1, :] for k in range(3))
            half = 0.5 * geom_ref[3, f : f + 1, :]
            along_h = nx * jump[0] + ny * jump[1] + nz * jump[2]
            along_e = nx * jump[3] + ny * jump[4] + nz * jump[5]
            flux[0].append(half * (nz * jump[4] - ny * jump[5] + jump[0] - along_h * nx))
            flux[1].append(half * (nx * jump[5] - nz * jump[3] + jump[1] - along_h * ny))
            flux[2].append(half * (ny * jump[3] - nx * jump[4] + jump[2] - along_h * nz))
            flux[3].append(half * (ny * jump[2] - nz * jump[1] + jump[3] - along_e * nx))
            flux[4].append(half * (nz * jump[0] - nx * jump[2] + jump[4] - along_e * ny))
            flux[5].append(half * (nx * jump[1] - ny * jump[0] + jump[5] - along_e * nz))
        for c in range(6):
            high, low = halves(jnp.concatenate(flux[c], axis=0))
            if step == 1:
                flux_high[c] = high
                flux_low[c] = low
            else:
                register = TIME_STEP * ((volume[c] + lifted(lift_ref[...], high, low)) * scale[...])
                reg_ref[c] = register
                adv_ref[c] = adv_ref[c] + RK_B[0] * register

    for step in range(2):
        for o in range(3):

            def sent(o=o, step=step):
                for j in peers(o):
                    copy(step, o, j).wait_send()

            guarded(send_ok[o], sent)


def finish(
    adv_ref, reg_ref, volume, scale, flux_high, flux_low, lift_ref, adv_hbm, reg_hbm, adv_out, reg_out, sem
):
    writes = []
    for c in range(6):
        register = TIME_STEP * ((volume[c] + lifted(lift_ref[...], flux_high[c], flux_low[c])) * scale[...])
        register = RK_A[1] * reg_ref[c] + register
        reg_out[c] = register
        adv_out[c] = adv_ref[c] + RK_B[1] * register
        for k, (src, dst) in enumerate(((reg_out, reg_hbm), (adv_out, adv_hbm))):
            write = pltpu.make_async_copy(src.at[c], dst.at[c], sem.at[k, c])
            write.start()
            writes.append(write)
    for write in writes:
        write.wait()


def on_device(
    n_dom,
    n_sub,
    fields,
    metric,
    face_geom,
    jacobian_ratio,
    curved,
    derivatives,
    lift_matrix,
    live_count,
    send_list,
    face_source,
    face_permutation,
):
    elements = fields.shape[2]
    faces = 4 * elements
    slots = 3 * n_sub * send_list.shape[3]
    vmem = pl.BlockSpec(memory_space=pltpu.VMEM)
    hbm = pl.BlockSpec(memory_space=pltpu.HBM)
    pick, spread, turn, pack, unpack = zero_one_matrices()
    operands = (
        fields,
        send_list.reshape(send_list.shape[1:]),
        pick,
        pack,
        face_source,
        derivatives,
        metric,
        curved.reshape(1, elements),
        jacobian_ratio,
        unpack,
        turn,
        face_permutation,
        face_geom,
        lift_matrix,
        spread,
    )
    operands = [pltpu.with_memory_space_constraint(a, pltpu.HBM) for a in operands]
    held = [pltpu.VMEM(a.shape, a.dtype) for a in operands[1:]]
    whole = jax.ShapeDtypeStruct(fields.shape, F32)
    flux = jax.ShapeDtypeStruct((6, 4 * ROWS, elements), BF16)
    carried = pl.pallas_call(
        functools.partial(kernel, n_dom, n_sub),
        out_shape=(
            whole,
            whole,
            whole,
            jax.ShapeDtypeStruct((NODES, elements), F32),
            flux,
            flux,
            jax.ShapeDtypeStruct((2 * NODES, 4 * ROWS), BF16),
        ),
        in_specs=[pl.BlockSpec(memory_space=pltpu.SMEM)] + [hbm] * 15,
        out_specs=(vmem,) * 7,
        scratch_shapes=held
        + [
            pltpu.VMEM((2 * PAIR, faces), BF16),
            pltpu.VMEM((2, 4, GROUP, elements), F32),
            pltpu.VMEM((2 * PAIR, faces), F32),
            pltpu.VMEM((faces, faces), BF16),
            pltpu.VMEM((slots, faces), BF16),
            pltpu.VMEM((slots, faces), BF16),
            pltpu.VMEM((2, slots, LANES), F32),
            pltpu.VMEM((2, slots, LANES), F32),
            pltpu.SemaphoreType.DMA((15,)),
            pltpu.SemaphoreType.DMA((2, 3, n_sub)),
            pltpu.SemaphoreType.DMA((2, 3, n_sub)),
        ],
        compiler_params=pltpu.CompilerParams(
            collective_id=0, has_side_effects=True, vmem_limit_bytes=40 * 1024 * 1024
        ),
        cost_estimate=pl.CostEstimate(flops=4_000_000_000, bytes_accessed=2_000_000, transcendentals=0),
    )(live_count, *operands)
    return pl.pallas_call(
        finish,
        out_shape=(whole, whole),
        in_specs=[vmem] * 7,
        out_specs=(hbm, hbm),
        scratch_shapes=[
            pltpu.VMEM(fields.shape, F32),
            pltpu.VMEM(fields.shape, F32),
            pltpu.SemaphoreType.DMA((2, 6)),
        ],
        compiler_params=pltpu.CompilerParams(vmem_limit_bytes=40 * 1024 * 1024),
        cost_estimate=pl.CostEstimate(flops=100_000_000, bytes_accessed=2_000_000, transcendentals=0),
    )(*carried)


def solution(mesh):
    return jax.shard_map(
        functools.partial(on_device, mesh.shape["dom"], mesh.shape["sub"]),
        mesh=mesh,
        in_specs=(
            P(None, None, ("dom", "sub")),
            P(None, ("dom", "sub")),
            P(None, None, ("dom", "sub")),
            P(None, ("dom", "sub")),
            P(("dom", "sub")),
            P(),
            P(),
            P(("dom", "sub")),
            P(("dom", "sub"), None, None, None),
            P(None, ("dom", "sub")),
            P(None, ("dom", "sub")),
        ),
        out_specs=(P(None, None, ("dom", "sub")), P(None, None, ("dom", "sub"))),
        check_vma=False,
    )
```
